512 devices in a mesh: segment: 2 (over core), band: 64 (over x, z_hi, y), chan: 4 (over z_lo).
Axes of the slice: x: 4, y: 4, z: 16 (z_hi: 4, z_lo: 4; z = z_hi * 4 + z_lo), core: 2. Of those that a mesh axis runs over, the one named last changes fastest.
Arguments:
- hidden_states: bfloat16 [4, 64, 64, 5120], P('segment', 'band', None, 'chan')
- modulation_shift: float32 [5120], P('chan'), may hold values from -3 to 3
- modulation_scale: float32 [5120], P('chan'), may hold values from -2.5 to 2.5
- head_weight: bfloat16 [5120, 64], P('chan'), may hold values from -0.078125 to 0.078125
- entry_weight: bfloat16 [3, 3, 3, 384, 16], P(None, None, None, 'chan')
- first_weight: bfloat16 [3, 3, 3, 384, 384], P(None, None, None, 'chan')
- first_gain: float32 [384], P('chan'), may hold values from 0.25 to 1.75
- second_weight: bfloat16 [3, 3, 3, 384, 384], P(None, None, None, 'chan'), may hold values from -0.0625 to 0.0625
- second_gain: float32 [384], P('chan'), may hold values from 0.25 to 1.75
Outputs:
- decoded: bfloat16 [384, 4, 128, 128], P('chan', 'segment', 'band')
The draws below stay inside these ranges and needn't reach their ends.
All inputs are finite; a program needn't handle non-finite values.
Results may differ from the reference program's by a relative error of at most 0.0075.
Values may be sent and summed in bfloat16 or wider, within the bound.
A program may use at most 128 MiB of HBM per device.

```python
import math
import jax
import jax.numpy as jnp
from jax import lax

D = 5120
ZC = 16
C = 384
TLAT = 4
HTOK = 64
WTOK = 64


def channel_scales(key, count):
    order = jnp.arange(count, dtype=jnp.float32) / (count - 1)
    spread = jax.random.uniform(key, (count,), jnp.float32)
    return jnp.exp(math.log(3.0) * (order - 0.5) + math.log(10.0) * (spread - 0.5))


def rough_values(key, shape):
    return jax.random.normal(key, shape, jnp.float32)


def draw_hidden_states(key, part):
    key = jax.random.fold_in(key, 7)
    value_key, scale_key = jax.random.split(key, 2)
    shape = (TLAT, HTOK, WTOK, D)
    factors = channel_scales(scale_key, D)
    values = rough_values(value_key, shape)
    return (values * factors).astype(jnp.bfloat16)


def draw_entry_weight(key, part):
    key = jax.random.fold_in(key, 11)
    value_key, scale_key = jax.random.split(key)
    shape = (3, 3, 3, C, ZC)
    values = rough_values(value_key, shape)
    factors = channel_scales(scale_key, C)
    return (values * factors[:, None] / math.sqrt(27.0 * ZC)).astype(jnp.bfloat16)


def draw_first_weight(key, part):
    key = jax.random.fold_in(key, 13)
    value_key, scale_key = jax.random.split(key)
    shape = (3, 3, 3, C, C)
    values = rough_values(value_key, shape)
    factors = channel_scales(scale_key, C)
    return (values * factors[:, None] / math.sqrt(27.0 * C)).astype(jnp.bfloat16)


def shard_levels(key, dims, cuts, smallest, high):
    level = 1.0
    for axis_at, blocks in cuts:
        draws = jax.random.uniform(jax.random.fold_in(jax.random.fold_in(key, 6), axis_at), (blocks,), jnp.float32, smallest / len(cuts), high / len(cuts))
        level = level * jnp.repeat(jnp.exp(draws), dims[axis_at] // blocks).reshape((-1,) + (1,) * (len(dims) - 1 - axis_at))
    return level


def bell_draw(key, dims, scale, most, cuts=(), kind=jnp.bfloat16):
    level = shard_levels(key, dims, cuts, -0.22, 0.18) if cuts else 1.0
    array = jax.random.normal(key, dims, jnp.float32) * scale * level
    return jnp.minimum(jnp.maximum(array, -most), most).astype(kind)


def setup_inputs(seed: int = 0) -> dict:
    streams_of = jax.random.split(jax.random.key(seed), 10)
    return {
        "hidden_states": draw_hidden_states(jax.random.fold_in(streams_of[9], 71), 0),
        "modulation_shift": bell_draw(streams_of[1], (D,), 0.5, 3.0, ((0, 4),), jnp.float32),
        "modulation_scale": bell_draw(streams_of[2], (D,), 0.3, 2.5, ((0, 4),), jnp.float32),
        "head_weight": bell_draw(streams_of[3], (D, 4 * ZC), D ** -0.5, 0.078125, ((0, 4),)),
        "entry_weight": draw_entry_weight(jax.random.fold_in(streams_of[9], 71), 0),
        "first_weight": draw_first_weight(jax.random.fold_in(streams_of[9], 71), 0),
        "first_gain": jnp.clip(1.0 + 0.15 * jax.random.normal(streams_of[6], (C,), jnp.float32), 0.25, 1.75),
        "second_weight": bell_draw(streams_of[7], (3, 3, 3, C, C), (27 * C) ** -0.5, 0.0625, ((3, 4),)),
        "second_gain": jnp.clip(1.0 + 0.15 * jax.random.normal(streams_of[8], (C,), jnp.float32), 0.25, 1.75),
    }


def causal_conv(inputs, weight):
    channels, frames, height, columns = inputs.shape
    padded = jnp.pad(inputs, ((0, 0), (2, 0), (1, 1), (1, 1)))
    summed = jnp.zeros((weight.shape[3], frames * height * columns), jnp.float32)
    for tap_time in range(3):
        for tap_row in range(3):
            for tap_col in range(3):
                window = padded[:, tap_time:tap_time + frames, tap_row:tap_row + height, tap_col:tap_col + columns]
                summed = summed + jnp.dot(weight[tap_time, tap_row, tap_col], window.reshape(channels, -1), preferred_element_type=jnp.float32)
    return summed.reshape(weight.shape[3], frames, height, columns)

def norm_silu(values, gain):
    wide = values.astype(jnp.float32)
    power = lax.optimization_barrier(jnp.mean(wide * wide, axis=0, keepdims=True))
    scaled = wide * lax.rsqrt(power + 1e-06) * gain[:, None, None, None]
    return jax.nn.silu(scaled).astype(jnp.bfloat16)

def reference(hidden_states, modulation_shift, modulation_scale, head_weight, entry_weight, first_weight, first_gain, second_weight, second_gain):
    states = hidden_states.astype(jnp.float32)
    center = lax.optimization_barrier(jnp.mean(states, axis=-1, keepdims=True))
    spread = lax.optimization_barrier(jnp.mean(states * states, axis=-1, keepdims=True)) - center * center
    normed = (states - center) * lax.rsqrt(spread + 1e-06) * (1.0 + modulation_scale) + modulation_shift
    head = jnp.einsum('thwd,dk->thwk', normed, head_weight.astype(jnp.float32), precision=lax.Precision.HIGHEST).astype(jnp.bfloat16)
    frames, token_rows, token_cols = (head.shape[0], head.shape[1], head.shape[2])
    latent = head.reshape(frames, token_rows, token_cols, ZC, 2, 2).transpose(3, 0, 1, 4, 2, 5).reshape(ZC, frames, 2 * token_rows, 2 * token_cols)
    entry = causal_conv(latent, entry_weight).astype(jnp.bfloat16)
    first_act = norm_silu(entry, first_gain)
    middle = causal_conv(first_act, first_weight).astype(jnp.bfloat16)
    second_act = norm_silu(middle, second_gain)
    return (entry.astype(jnp.float32) + causal_conv(second_act, second_weight)).astype(jnp.bfloat16)
```

```python
import jax
import jax.numpy as jnp
from jax import lax
from jax.experimental import pallas as pl
from jax.experimental.pallas import tpu as pltpu
from jax.sharding import PartitionSpec as P

D = 5120
C = 384
EPS = 1e-6
OWN = 96
X = 128
MESH = pl.DeviceIdType.MESH
NT = (((1,), (1,)), ((), ()))
F32 = jnp.float32
BF16 = jnp.bfloat16


def iota(shape, axis):
    return lax.broadcasted_iota(jnp.int32, shape, axis)


def column(row, rows):
    eye = iota((rows, X), 0) == iota((rows, X), 1)
    return jnp.sum(jnp.where(eye, jnp.broadcast_to(row, (rows, X)), 0.0), axis=1, keepdims=True)


def as_row(col):
    rows = col.shape[0]
    eye = iota((rows, X), 0) == iota((rows, X), 1)
    return jnp.sum(jnp.where(eye, jnp.broadcast_to(col, (rows, X)), 0.0), axis=0, keepdims=True)


def silu_norm(values, gain):
    power = jnp.sum(values * values, axis=0, keepdims=True) / C
    scaled = values * lax.rsqrt(power + EPS) * gain
    return (scaled * (0.5 * jnp.tanh(0.5 * scaled) + 0.5)).astype(BF16)


def kernel(
    h_ref, shift_ref, scale_ref, wt_ref, ew_ref, w1_hbm, g1_ref, w2_hbm, g2_ref,
    out_ref,
    w1, w2, parts, ewg, ewp, lat, cols, act1, raw, act2, total, gains, resid, fin,
    wsem, s_p, r_p, s_e, r_e, s_es, r_es, s_l, r_l, s_g, r_g, s_o, r_o, s_h, r_h, s_s, r_s, s_f, r_f,
):
    s, b, c = lax.axis_index("segment"), lax.axis_index("band"), lax.axis_index("chan")
    bands = lax.axis_size("band")
    up, down = lax.rem(b + 1, bands), lax.rem(b + bands - 1, bands)
    zpeers = [(s, b, lax.rem(c + d, 4)) for d in (1, 2, 3)]
    sibling = (1 - s, b, c)
    outer = (1 - s, jnp.where(s == 0, down, up), c)
    far = [(s, up, c), (1 - s, up, c), (s, down, c), (1 - s, down, c)]

    barrier = pltpu.get_barrier_semaphore()
    for peer in zpeers + [sibling] + far:
        pl.semaphore_signal(barrier, inc=1, device_id=peer, device_id_type=MESH)
    load1 = pltpu.make_async_copy(w1_hbm, w1, wsem.at[0])
    load2 = pltpu.make_async_copy(w2_hbm, w2, wsem.at[1])
    load1.start()
    load2.start()

    def remote(src, dst, send, recv, peer):
        copy = pltpu.make_async_remote_copy(
            src_ref=src, dst_ref=dst, send_sem=send, recv_sem=recv, device_id=peer, device_id_type=MESH
        )
        copy.start()
        return copy

    sent = []

    order = iota((64, 64), 0)
    source = 4 * lax.rem(order, 16) + 2 * lax.rem(order // 16, 2) + order // 32
    permute = (iota((64, 64), 1) == source).astype(F32).astype(BF16)
    weight = jnp.dot(permute, wt_ref[...], preferred_element_type=F32)
    raised = weight * (1.0 + scale_ref[...])
    high = raised.astype(BF16)
    low = (raised - high.astype(F32)).astype(BF16)
    both = lax.dot_general(jnp.concatenate([high, low], axis=0), h_ref[...], NT, preferred_element_type=F32)
    states = h_ref[...].astype(F32)
    parts[c] = jnp.zeros((72, X), F32)
    parts[c, 0:64, :] = both[0:64] + both[64:128]
    parts[c, 64:65, :] = as_row(jnp.sum(states, axis=1, keepdims=True))
    parts[c, 65:66, :] = as_row(jnp.sum(states * states, axis=1, keepdims=True))
    parts[c, 66:67, :] = as_row(jnp.sum(high.astype(F32) + low.astype(F32), axis=1, keepdims=True))
    parts[c, 67:68, :] = as_row(jnp.sum(weight * shift_ref[...], axis=1, keepdims=True))
    parts[c, 68:69, 0:OWN] = g1_ref[...]
    parts[c, 69:70, 0:OWN] = g2_ref[...]

    pl.semaphore_wait(barrier, 8)
    first = [remote(parts.at[c], parts.at[c], s_p.at[d], r_p.at[d], zpeers[d]) for d in range(3)]
    sent += first

    own_rows = pl.ds(pl.multiple_of(c * OWN, OWN), OWN)
    ewp[0:432, :] = ew_ref[...]
    ewp[432:512, :] = jnp.zeros((80, OWN), BF16)
    eye96 = (iota((OWN, OWN), 0) == iota((OWN, OWN), 1)).astype(F32).astype(BF16)
    half = ewp[pl.ds(pl.multiple_of(s * 256, 256), 256), :]
    ewg[s, own_rows, :] = lax.dot_general(eye96, half, NT, preferred_element_type=F32).astype(BF16)
    gather_e = [
        remote(ewg.at[s, own_rows], ewg.at[s, own_rows], s_e.at[d], r_e.at[d], zpeers[d]) for d in range(3)
    ]
    sent += gather_e

    zero = jnp.zeros((16, X), BF16)
    for e in range(3):
        for f in range(4):
            at = (e * 4 + f) * X
            cols[432:512, at : at + X] = jnp.zeros((80, X), BF16)
            for p in range(2 - f):
                for qr in range(9):
                    k = (p * 9 + qr) * 16
                    cols[k : k + 16, at : at + X] = zero
        act1[e, :, 0:X] = jnp.zeros((C, X), BF16)
        act2[e, :, 0:X] = jnp.zeros((C, X), BF16)

    for copy in first:
        copy.wait_recv()
    summed = (parts[0] + parts[1]) + (parts[2] + parts[3])
    center = summed[64:65] / D
    spread = summed[65:66] / D - center * center
    head = (summed[0:64] - column(summed[66:67], 64) * center) * lax.rsqrt(spread + EPS) + column(
        summed[67:68], 64
    )
    head = head.astype(BF16)
    even = lax.rem(iota((32, X), 1), 2) == 0
    for t in range(2):
        spreadout = (iota((X, X), 0) == t * 64 + iota((X, X), 1) // 2).astype(F32).astype(BF16)
        wide = jnp.dot(head, spreadout, preferred_element_type=F32)
        lat[1, 2 * s + t] = jnp.where(even, wide[0:32], wide[32:64]).astype(BF16)
    mine = pl.ds(2 * s, 2)
    latents = [remote(lat.at[1, mine], lat.at[1, mine], s_l.at[0], r_l.at[0], sibling)]
    for j, peer in enumerate(far):
        latents.append(
            remote(lat.at[1, mine], lat.at[0 if j < 2 else 2, mine], s_l.at[1 + j], r_l.at[1 + j], peer)
        )
    sent += latents
    for chan in range(4):
        for g in range(2):
            row = parts[chan, 68 + g : 69 + g, :]
            gains[g, chan * OWN : (chan + 1) * OWN, :] = jnp.broadcast_to(column(row, OWN), (OWN, X))

    for copy in gather_e:
        copy.wait_recv()
    share = remote(ewg.at[s], ewg.at[s], s_es, r_es, sibling)
    sent.append(share)
    for copy in latents:
        copy.wait_recv()

    @pl.when(b == 0)
    def _():
        lat[0] = jnp.zeros((4, 32, X), BF16)

    @pl.when(b == bands - 1)
    def _():
        lat[2] = jnp.zeros((4, 32, X), BF16)

    lane = iota((16, X), 1)
    for k in range(5):
        slot, a = (s + k) // 2, lax.rem(s + k, 2)
        for f in range(4):
            tile = lat[slot, f, pl.ds(pl.multiple_of(a * 16, 16), 16), :]
            wide = tile.astype(F32)
            shifted = [
                jnp.where(lane == 0, 0.0, pltpu.roll(wide, 1, 1)).astype(BF16),
                tile,
                jnp.where(lane == X - 1, 0.0, pltpu.roll(wide, X - 1, 1)).astype(BF16),
            ]
            for p in range(3):
                for q in range(3):
                    e, g = k - q, f + 2 - p
                    if 0 <= e < 3 and g < 4:
                        for r in range(3):
                            row = ((p * 3 + q) * 3 + r) * 16
                            at = (e * 4 + g) * X
                            cols[row : row + 16, at : at + X] = shifted[r]

    share.wait_recv()
    row_at = 2 * b + s
    for e in range(3):
        for pair in range(2):
            at = (e * 4 + pair * 2) * X
            value = jnp.dot(ewg[0], cols[0:256, at : at + 2 * X], preferred_element_type=F32)
            value += jnp.dot(ewg[1], cols[256:512, at : at + 2 * X], preferred_element_type=F32)
            rounded = value.astype(BF16)
            if e == 1:
                total[0, :, 0 : 2 * X] = rounded.astype(F32)
                resid[:, pair * 2 * X : (pair + 1) * 2 * X] = total[0, own_rows, 0 : 2 * X]
            valid = (row_at + e - 1 >= 0) & (row_at + e - 1 < 2 * bands)
            for t in range(2):
                done = silu_norm(rounded[:, t * X : (t + 1) * X].astype(F32), gains[0])
                lanes = (pair * 2 + t + 1) * X
                act1[e, :, lanes : lanes + X] = jnp.where(valid, done, jnp.zeros_like(done))

    def taps(weights, acts, q, pair):
        value = None
        for p in range(1 if pair == 0 else 0, 3):
            lanes = (pair * 2 + p - 1) * X
            rows = pl.ds(pl.multiple_of((p * 3 + q) * 288, 288), 288)
            term = jnp.dot(weights[rows, :], acts[q, :, lanes : lanes + 2 * X], preferred_element_type=F32)
            value = term if value is None else value + term
        return value

    lane96 = iota((OWN, X), 1)

    def join(value, t):
        lanes = slice(t * X, (t + 1) * X)
        left = jnp.where(lane96 == 0, 0.0, pltpu.roll(value[0:OWN, lanes], 1, 1))
        right = jnp.where(lane96 == X - 1, 0.0, pltpu.roll(value[2 * OWN : 3 * OWN, lanes], X - 1, 1))
        return left + value[OWN : 2 * OWN, lanes] + right

    near, away = 2 - 2 * s, 2 * s
    load1.wait()
    own_gather, across = [], []
    for pair in range(2):
        value = taps(w1, act1, 0, pair) + taps(w1, act1, 1, pair) + taps(w1, act1, 2, pair)
        for t in range(2):
            f = pair * 2 + t
            raw[1, f, own_rows, :] = join(value, t).astype(BF16)
            tile = raw.at[1, f, own_rows]
            across.append(remote(tile, raw.at[near, f, own_rows], s_o.at[f], r_o.at[f], outer))
            own_gather.append(
                [remote(tile, tile, s_g.at[f, d], r_g.at[f, d], zpeers[d]) for d in range(3)]
            )

    def activate(slot, f, valid):
        done = silu_norm(raw[slot, f].astype(F32), gains[1])
        lanes = (f + 1) * X
        act2[slot, :, lanes : lanes + X] = jnp.where(valid, done, jnp.zeros_like(done))

    halo, to_sibling = [], []
    for f in range(4):
        for copy in own_gather[f]:
            copy.wait_recv()
        to_sibling.append(remote(raw.at[1, f], raw.at[away, f], s_s.at[f], r_s.at[f], sibling))
        across[f].wait_recv()
        tile = raw.at[away, f, own_rows]
        halo.append([remote(tile, tile, s_h.at[f, d], r_h.at[f, d], zpeers[d]) for d in range(3)])
        activate(1, f, True)
    load2.wait()
    for pair in range(2):
        total[pair, 0:288, 0 : 2 * X] = taps(w2, act2, 1, pair)
    for f in range(4):
        to_sibling[f].wait_recv()
        activate(near, f, True)
    for pair in range(2):
        total[pair, 0:288, 0 : 2 * X] += taps(w2, act2, near, pair)
    inside = jnp.where(s == 0, b > 0, b < bands - 1)
    finals = []
    for pair in range(2):
        for f in (2 * pair, 2 * pair + 1):
            for copy in halo[f]:
                copy.wait_recv()
            activate(away, f, inside)
        value = total[pair, 0:288, 0 : 2 * X] + taps(w2, act2, away, pair)
        for t in range(2):
            f = pair * 2 + t
            decoded = (resid[:, f * X : (f + 1) * X] + join(value, t)).astype(BF16)
            fin[0, f] = decoded
    sections = remote(
        fin.at[0, pl.ds(2 * (1 - s), 2)], fin.at[1, pl.ds(2 * (1 - s), 2)], s_f, r_f, sibling
    )
    sent.append(sections)
    for t in range(2):
        out_ref[t, s] = fin[0, 2 * s + t]
    sections.wait_recv()
    for t in range(2):
        out_ref[t, 1 - s] = fin[1, 2 * s + t]
    for group in own_gather + halo:
        sent += group
    for copy in sent + across + to_sibling:
        copy.wait_send()


def body(
    hidden_states, modulation_shift, modulation_scale, head_weight, entry_weight,
    first_weight, first_gain, second_weight, second_gain,
):
    vmem = pl.BlockSpec(memory_space=pltpu.VMEM)
    anywhere = pl.BlockSpec(memory_space=pl.ANY)
    dma = pltpu.SemaphoreType.DMA
    out = pl.pallas_call(
        kernel,
        out_shape=jax.ShapeDtypeStruct((2, 2, OWN, X), BF16),
        in_specs=[vmem] * 5 + [anywhere, vmem, anywhere, vmem],
        out_specs=vmem,
        scratch_shapes=[
            pltpu.VMEM((2592, C), BF16),
            pltpu.VMEM((2592, C), BF16),
            pltpu.VMEM((4, 72, X), F32),
            pltpu.VMEM((2, C, 256), BF16),
            pltpu.VMEM((512, OWN), BF16),
            pltpu.VMEM((3, 4, 32, X), BF16),
            pltpu.VMEM((512, 12 * X), BF16),
            pltpu.VMEM((3, C, 5 * X), BF16),
            pltpu.VMEM((3, 4, C, X), BF16),
            pltpu.VMEM((3, C, 5 * X), BF16),
            pltpu.VMEM((2, C, 2 * X), F32),
            pltpu.VMEM((2, C, X), F32),
            pltpu.VMEM((OWN, 4 * X), F32),
            pltpu.VMEM((2, 4, OWN, X), BF16),
            dma((2,)), dma((3,)), dma((3,)), dma((3,)), dma((3,)), dma, dma, dma((5,)), dma((5,)),
            dma((4, 3)), dma((4, 3)), dma((4,)), dma((4,)), dma((4, 3)), dma((4, 3)), dma((4,)), dma((4,)),
            dma, dma,
        ],
        compiler_params=pltpu.CompilerParams(
            collective_id=0, has_side_effects=True, vmem_limit_bytes=48 * 2**20
        ),
    )(
        hidden_states.reshape(128, 1280),
        modulation_shift.reshape(1, 1280),
        modulation_scale.reshape(1, 1280),
        head_weight.T,
        entry_weight.transpose(0, 1, 2, 4, 3).reshape(432, OWN),
        first_weight.reshape(2592, C),
        first_gain.reshape(1, OWN),
        second_weight.reshape(2592, C),
        second_gain.reshape(1, OWN),
    )
    return out.transpose(2, 0, 1, 3)


def solution(mesh):
    return jax.shard_map(
        body,
        mesh=mesh,
        in_specs=(
            P("segment", "band", None, "chan"),
            P("chan"),
            P("chan"),
            P("chan", None),
            P(None, None, None, "chan", None),
            P(None, None, None, "chan", None),
            P("chan"),
            P(None, None, None, "chan", None),
            P("chan"),
        ),
        out_specs=P("chan", "segment", "band", None),
        check_vma=False,
    )
```

```python
import jax
import jax.numpy as jnp
from jax import lax
from jax.experimental import pallas as pl
from jax.experimental.pallas import tpu as pltpu
from jax.sharding import PartitionSpec as P

D = 5120
C = 384
EPS = 1e-6
OWN = 96
X = 128
MESH = pl.DeviceIdType.MESH
NT = (((1,), (1,)), ((), ()))
F32 = jnp.float32
BF16 = jnp.bfloat16


def iota(shape, axis):
    return lax.broadcasted_iota(jnp.int32, shape, axis)


def column(row, rows):
    eye = iota((rows, X), 0) == iota((rows, X), 1)
    return jnp.sum(jnp.where(eye, jnp.broadcast_to(row, (rows, X)), 0.0), axis=1, keepdims=True)


def as_row(col):
    rows = col.shape[0]
    eye = iota((rows, X), 0) == iota((rows, X), 1)
    return jnp.sum(jnp.where(eye, jnp.broadcast_to(col, (rows, X)), 0.0), axis=0, keepdims=True)


def lanes_of(ref):
    return jnp.concatenate([ref[j : j + 1, :] for j in range(10)], axis=1)


def silu_norm(values, gain):
    power = jnp.sum(values * values, axis=0, keepdims=True) / C
    scaled = values * lax.rsqrt(power + EPS) * gain
    return (scaled * (0.5 * jnp.tanh(0.5 * scaled) + 0.5)).astype(BF16)


def kernel(
    h_hbm, shift_hbm, scale_hbm, wt_hbm, ew_hbm, w1_hbm, g1_hbm, w2_hbm, g2_hbm,
    out_ref,
    h_ref, shift_ref, scale_ref, wt_ref, g1_ref, g2_ref, w1, w2, parts, ewg, ewp, lat, cols, act1, raw, act2, total, gains, resid, fin,
    wsem, s_p, r_p, s_e, r_e, s_es, r_es, s_l, r_l, s_g, r_g, s_o, r_o, s_h, r_h, s_s, r_s, s_f, r_f,
):
    s, b, c = lax.axis_index("segment"), lax.axis_index("band"), lax.axis_index("chan")
    bands = lax.axis_size("band")
    up, down = lax.rem(b + 1, bands), lax.rem(b + bands - 1, bands)
    zpeers = [(s, b, lax.rem(c + d, 4)) for d in (1, 2, 3)]
    sibling = (1 - s, b, c)
    outer = (1 - s, jnp.where(s == 0, down, up), c)
    y = lax.rem(b, 4)
    apart = jnp.where(s == 0, y == 0, y == 3)
    passes = (y == 1) | (y == 2)
    goal = (2 - y, lax.rem(b + jnp.where(y == 2, 2, bands - 2), bands), c)
    skipped = lax.rem(b + jnp.where(s == 0, bands - 2, 2), bands)
    far = [(s, up, c), (1 - s, up, c), (s, down, c), (1 - s, down, c)]

    pairs = (
        (wt_hbm, wt_ref), (scale_hbm, scale_ref), (shift_hbm, shift_ref), (h_hbm, h_ref), (g1_hbm, g1_ref), (g2_hbm, g2_ref),
        (ew_hbm, ewp.at[pl.ds(0, 432)]), (w1_hbm, w1), (w2_hbm, w2),
    )
    loads = [pltpu.make_async_copy(src, dst, wsem.at[i]) for i, (src, dst) in enumerate(pairs)]
    for load in loads:
        load.start()
    barrier = pltpu.get_barrier_semaphore()
    for peer in zpeers + [sibling] + far:
        pl.semaphore_signal(barrier, inc=1, device_id=peer, device_id_type=MESH)

    @pl.when(apart)
    def _():
        for seg in range(2):
            pl.semaphore_signal(barrier, inc=1, device_id=(seg, skipped, c), device_id_type=MESH)


    def ready(src, dst, send, recv, peer):
        return pltpu.make_async_remote_copy(
            src_ref=src, dst_ref=dst, send_sem=send, recv_sem=recv, device_id=peer, device_id_type=MESH
        )

    def remote(*ends):
        copy = ready(*ends)
        copy.start()
        return copy

    sent = []

    order = iota((64, 64), 0)
    source = 4 * lax.rem(order, 16) + 2 * lax.rem(order // 16, 2) + order // 32
    permute = (iota((64, 64), 1) == source).astype(F32).astype(BF16)
    for load in loads[:3]:
        load.wait()
    weight = jnp.dot(permute, wt_ref[...], preferred_element_type=F32)
    raised = weight * (1.0 + lanes_of(scale_ref))
    high = raised.astype(BF16)
    low = (raised - high.astype(F32)).astype(BF16)
    for load in loads[3:6]:
        load.wait()
    both = lax.dot_general(jnp.concatenate([high, low], axis=0), h_ref[...], NT, preferred_element_type=F32)
    states = h_ref[...].astype(F32)
    parts[c] = jnp.zeros((72, X), F32)
    parts[c, 0:64, :] = both[0:64] + both[64:128]
    parts[c, 64:65, :] = as_row(jnp.sum(states, axis=1, keepdims=True))
    parts[c, 65:66, :] = as_row(jnp.sum(states * states, axis=1, keepdims=True))
    parts[c, 66:67, :] = as_row(jnp.sum(high.astype(F32) + low.astype(F32), axis=1, keepdims=True))
    parts[c, 67:68, :] = as_row(jnp.sum(weight * lanes_of(shift_ref), axis=1, keepdims=True))
    parts[c, 68:69, 0:OWN] = g1_ref[...]
    parts[c, 69:70, 0:OWN] = g2_ref[...]

    pl.semaphore_wait(barrier, 8 + passes.astype(jnp.int32))
    first = [remote(parts.at[c], parts.at[c], s_p.at[d], r_p.at[d], zpeers[d]) for d in range(3)]
    sent += first

    own_rows = pl.ds(pl.multiple_of(c * OWN, OWN), OWN)
    loads[6].wait()
    ewp[432:512, :] = jnp.zeros((80, OWN), BF16)
    eye96 = (iota((OWN, OWN), 0) == iota((OWN, OWN), 1)).astype(F32).astype(BF16)
    half = ewp[pl.ds(pl.multiple_of(s * 256, 256), 256), :]
    ewg[s, own_rows, :] = lax.dot_general(eye96, half, NT, preferred_element_type=F32).astype(BF16)
    gather_e = [
        remote(ewg.at[s, own_rows], ewg.at[s, own_rows], s_e.at[d], r_e.at[d], zpeers[d]) for d in range(3)
    ]
    sent += gather_e

    zero = jnp.zeros((16, X), BF16)
    for e in range(4):
        for f in range(4):
            at = (e * 4 + f) * X
            cols[432:512, at : at + X] = jnp.zeros((80, X), BF16)
            for p in range(2 - f):
                for qr in range(9):
                    k = (p * 9 + qr) * 16
                    cols[k : k + 16, at : at + X] = zero
        act1[e, :, 0:X] = jnp.zeros((C, X), BF16)
    for slot in range(3):
        act2[slot, :, 0:X] = jnp.zeros((C, X), BF16)

    @pl.when(~apart)
    def _():
        lat[4 * s] = jnp.zeros((4, 32, X), BF16)

    for copy in first:
        copy.wait_recv()
    summed = (parts[0] + parts[1]) + (parts[2] + parts[3])
    center = summed[64:65] / D
    spread = summed[65:66] / D - center * center
    head = (summed[0:64] - column(summed[66:67], 64) * center) * lax.rsqrt(spread + EPS) + column(
        summed[67:68], 64
    )
    head = head.astype(BF16)
    even = lax.rem(iota((32, X), 1), 2) == 0
    for t in range(2):
        spreadout = (iota((X, X), 0) == t * 64 + iota((X, X), 1) // 2).astype(F32).astype(BF16)
        wide = jnp.dot(head, spreadout, preferred_element_type=F32)
        lat[2, 2 * s + t] = jnp.where(even, wide[0:32], wide[32:64]).astype(BF16)
    mine = pl.ds(2 * s, 2)
    whole, row0, row1 = pl.ds(0, 32), pl.ds(0, 16), pl.ds(16, 16)

    def latent(slot, rows, j, arrives, peer):
        return ready(lat.at[2, mine, rows], lat.at[slot, mine, rows], s_l.at[j], r_l.at[arrives], peer)

    latents = [
        latent(1, whole, 1, 1 + s, (0, up, c)),
        latent(1, row1, 2, 1 + s, (1, up, c)),
        latent(3, row0, 3, 3 + s, (0, down, c)),
        latent(3, whole, 4, 3 + s, (1, down, c)),
        latent(2, whole, 0, 0, sibling),
    ]
    beyond = (latent(0, row1, 5, 5 + s, goal), latent(4, row0, 5, 5 + s, goal))
    for seg in range(2):
        pl.when(passes & (goal[0] == seg))(beyond[seg].start)
    for copy in latents:
        copy.start()
    sent += latents
    for chan in range(4):
        for g in range(2):
            row = parts[chan, 68 + g : 69 + g, :]
            gains[g, chan * OWN : (chan + 1) * OWN, :] = jnp.broadcast_to(column(row, OWN), (OWN, X))

    for copy in gather_e:
        copy.wait_recv()
    share = remote(ewg.at[s], ewg.at[s], s_es, r_es, sibling)
    sent.append(share)
    latents[4].wait_recv()
    for seg in range(2):

        @pl.when(s == seg)
        def _():
            for slot, rows in ((1, (whole, row1)[seg]), (3, (row0, whole)[seg])):
                for source_seg in range(2):
                    latent(slot, rows, 1, slot + source_seg, sibling).wait_recv()

        @pl.when(apart & (s == seg))
        def _():
            for source_seg in range(2):
                latent(4 * seg, (row1, row0)[seg], 5, 5 + source_seg, sibling).wait_recv()


    @pl.when(b == 0)
    def _():
        lat[1] = jnp.zeros((4, 32, X), BF16)

    @pl.when(b == bands - 1)
    def _():
        lat[3] = jnp.zeros((4, 32, X), BF16)

    lane = iota((16, X), 1)
    for k in range(6):
        slot, a = s + (1 + k) // 2, (1 + k) % 2
        for f in range(4):
            tile = lat[slot, f, a * 16 : a * 16 + 16, :]
            wide = tile.astype(F32)
            shifted = [
                jnp.where(lane == 0, 0.0, pltpu.roll(wide, 1, 1)).astype(BF16),
                tile,
                jnp.where(lane == X - 1, 0.0, pltpu.roll(wide, X - 1, 1)).astype(BF16),
            ]
            for p in range(3):
                for q in range(3):
                    e, g = k - q, f + 2 - p
                    if 0 <= e < 4 and g < 4:
                        for r in range(3):
                            row = ((p * 3 + q) * 3 + r) * 16
                            at = (e * 4 + g) * X
                            cols[row : row + 16, at : at + X] = shifted[r]

    share.wait_recv()
    row_at = 2 * b + 2 * s - 2
    for e in range(4):
        for pair in range(2):
            at = (e * 4 + pair * 2) * X
            value = jnp.dot(ewg[0], cols[0:256, at : at + 2 * X], preferred_element_type=F32)
            value += jnp.dot(ewg[1], cols[256:512, at : at + 2 * X], preferred_element_type=F32)
            rounded = value.astype(BF16)
            if e in (1, 2):

                @pl.when(s == 2 - e)
                def _():
                    total[0, :, 0 : 2 * X] = rounded.astype(F32)
                    resid[:, pair * 2 * X : (pair + 1) * 2 * X] = total[0, own_rows, 0 : 2 * X]

            valid = (row_at + e >= 0) & (row_at + e < 2 * bands)
            for t in range(2):
                done = silu_norm(rounded[:, t * X : (t + 1) * X].astype(F32), gains[0])
                lanes = (pair * 2 + t + 1) * X
                act1[e, :, lanes : lanes + X] = jnp.where(valid, done, jnp.zeros_like(done))

    def taps(weights, acts, q, pair, slot=None):
        slot = q if slot is None else slot
        value = None
        for p in range(1 if pair == 0 else 0, 3):
            lanes = (pair * 2 + p - 1) * X
            rows = pl.ds(pl.multiple_of((p * 3 + q) * 288, 288), 288)
            term = jnp.dot(weights[rows, :], acts[slot, :, lanes : lanes + 2 * X], preferred_element_type=F32)
            value = term if value is None else value + term
        return value

    lane96 = iota((OWN, X), 1)

    def join(value, t):
        lanes = slice(t * X, (t + 1) * X)
        left = jnp.where(lane96 == 0, 0.0, pltpu.roll(value[0:OWN, lanes], 1, 1))
        right = jnp.where(lane96 == X - 1, 0.0, pltpu.roll(value[2 * OWN : 3 * OWN, lanes], X - 1, 1))
        return left + value[OWN : 2 * OWN, lanes] + right

    near, away = 2 - 2 * s, 2 * s
    loads[7].wait()
    own_gather, across, halo, to_sibling = [], [], [], []
    for f in range(4):
        tile, passed = raw.at[1, f, own_rows], raw.at[away, f, own_rows]
        own_gather.append([ready(tile, tile, s_g.at[f, d], r_g.at[f, d], zpeers[d]) for d in range(3)])
        halo.append([ready(passed, passed, s_h.at[f, d], r_h.at[f, d], zpeers[d]) for d in range(3)])
        to_sibling.append(ready(raw.at[1, f], raw.at[away, f], s_s.at[f], r_s.at[f], sibling))
        across.append(ready(raw.at[1, f], raw.at[near, f], s_o.at[f], r_o.at[f], outer))

    def middle_row(start, slot, copies):
        for pair in range(2):
            value = None
            for q in range(3):
                term = taps(w1, act1, q, pair, start + q)
                value = term if value is None else value + term
            for t in range(2):
                f = pair * 2 + t
                raw[slot, f, own_rows, :] = join(value, t).astype(BF16)
                for copy in copies[f]:
                    copy.start()

    middle_row(1 - s, 1, own_gather)

    @pl.when(apart)
    def _():
        middle_row(s, away, halo)

    def activate(slot, f, valid):
        done = silu_norm(raw[slot, f].astype(F32), gains[1])
        lanes = (f + 1) * X
        act2[slot, :, lanes : lanes + X] = jnp.where(valid, done, jnp.zeros_like(done))

    for f in range(4):
        for copy in own_gather[f]:
            copy.wait_recv()
        to_sibling[f].start()
        pl.when(~apart)(across[f].start)
        activate(1, f, True)
    loads[8].wait()
    for pair in range(2):
        total[pair, 0:288, 0 : 2 * X] = taps(w2, act2, 1, pair)
    for f in range(4):
        to_sibling[f].wait_recv()
        activate(near, f, True)
    for pair in range(2):
        total[pair, 0:288, 0 : 2 * X] += taps(w2, act2, near, pair)
    inside = jnp.where(s == 0, b > 0, b < bands - 1)
    finals = []
    for pair in range(2):
        for f in (2 * pair, 2 * pair + 1):

            @pl.when(apart)
            def _():
                for copy in halo[f]:
                    copy.wait_recv()

            pl.when(~apart)(across[f].wait_recv)
            activate(away, f, inside)
        value = total[pair, 0:288, 0 : 2 * X] + taps(w2, act2, away, pair)
        for t in range(2):
            f = pair * 2 + t
            decoded = (resid[:, f * X : (f + 1) * X] + join(value, t)).astype(BF16)
            fin[0, f] = decoded
    sections = remote(
        fin.at[0, pl.ds(2 * (1 - s), 2)], fin.at[1, pl.ds(2 * (1 - s), 2)], s_f, r_f, sibling
    )
    sent.append(sections)
    for t in range(2):
        out_ref[t, s] = fin[0, 2 * s + t]
    sections.wait_recv()
    for t in range(2):
        out_ref[t, 1 - s] = fin[1, 2 * s + t]
    for seg in range(2):
        pl.when(passes & (goal[0] == seg))(beyond[seg].wait_send)
    for copy in sent + sum(own_gather, []) + to_sibling:
        copy.wait_send()

    @pl.when(apart)
    def _():
        for copy in sum(halo, []):
            copy.wait_send()

    @pl.when(~apart)
    def _():
        for copy in across:
            copy.wait_send()


def body(
    hidden_states, modulation_shift, modulation_scale, head_weight, entry_weight,
    first_weight, first_gain, second_weight, second_gain,
):
    vmem = pl.BlockSpec(memory_space=pltpu.VMEM)
    hbm = pl.BlockSpec(memory_space=pltpu.HBM)
    dma = pltpu.SemaphoreType.DMA
    out = pl.pallas_call(
        kernel,
        out_shape=jax.ShapeDtypeStruct((2, 2, OWN, X), BF16),
        in_specs=[hbm] * 9,
        out_specs=vmem,
        scratch_shapes=[
            pltpu.VMEM((128, 1280), BF16),
            pltpu.VMEM((10, X), F32),
            pltpu.VMEM((10, X), F32),
            pltpu.VMEM((64, 1280), BF16),
            pltpu.VMEM((1, OWN), F32),
            pltpu.VMEM((1, OWN), F32),
            pltpu.VMEM((2592, C), BF16),
            pltpu.VMEM((2592, C), BF16),
            pltpu.VMEM((4, 72, X), F32),
            pltpu.VMEM((2, C, 256), BF16),
            pltpu.VMEM((512, OWN), BF16),
            pltpu.VMEM((5, 4, 32, X), BF16),
            pltpu.VMEM((512, 16 * X), BF16),
            pltpu.VMEM((4, C, 5 * X), BF16),
            pltpu.VMEM((3, 4, C, X), BF16),
            pltpu.VMEM((3, C, 5 * X), BF16),
            pltpu.VMEM((2, C, 2 * X), F32),
            pltpu.VMEM((2, C, X), F32),
            pltpu.VMEM((OWN, 4 * X), F32),
            pltpu.VMEM((2, 4, OWN, X), BF16),
            dma((9,)), dma((3,)), dma((3,)), dma((3,)), dma((3,)), dma, dma, dma((6,)), dma((7,)),
            dma((4, 3)), dma((4, 3)), dma((4,)), dma((4,)), dma((4, 3)), dma((4, 3)), dma((4,)), dma((4,)),
            dma, dma,
        ],
        compiler_params=pltpu.CompilerParams(
            collective_id=0, has_side_effects=True, vmem_limit_bytes=63 * 2**20
        ),
    )(
        hidden_states.reshape(128, 1280),
        modulation_shift.reshape(10, X),
        modulation_scale.reshape(10, X),
        head_weight.T,
        entry_weight.transpose(0, 1, 2, 4, 3).reshape(432, OWN),
        first_weight.reshape(2592, C),
        first_gain.reshape(1, OWN),
        second_weight.reshape(2592, C),
        second_gain.reshape(1, OWN),
    )
    return out.transpose(2, 0, 1, 3)


def solution(mesh):
    return jax.shard_map(
        body,
        mesh=mesh,
        in_specs=(
            P("segment", "band", None, "chan"),
            P("chan"),
            P("chan"),
            P("chan", None),
            P(None, None, None, "chan", None),
            P(None, None, None, "chan", None),
            P("chan"),
            P(None, None, None, "chan", None),
            P("chan"),
        ),
        out_specs=P("chan", "segment", "band", None),
        check_vma=False,
    )
```

```python
import jax
import jax.numpy as jnp
from jax import lax
from jax.experimental import pallas as pl
from jax.experimental.pallas import tpu as pltpu
from jax.sharding import PartitionSpec as P

D = 5120
C = 384
EPS = 1e-6
OWN = 96
X = 128
MESH = pl.DeviceIdType.MESH
NT = (((1,), (1,)), ((), ()))
F32 = jnp.float32
BF16 = jnp.bfloat16


def iota(shape, axis):
    return lax.broadcasted_iota(jnp.int32, shape, axis)


def column(row, rows):
    eye = iota((rows, X), 0) == iota((rows, X), 1)
    return jnp.sum(jnp.where(eye, jnp.broadcast_to(row, (rows, X)), 0.0), axis=1, keepdims=True)


def as_row(col):
    rows = col.shape[0]
    eye = iota((rows, X), 0) == iota((rows, X), 1)
    return jnp.sum(jnp.where(eye, jnp.broadcast_to(col, (rows, X)), 0.0), axis=0, keepdims=True)


def lanes_of(ref):
    return jnp.concatenate([ref[j : j + 1, :] for j in range(10)], axis=1)


def silu_norm(values, gain):
    power = jnp.sum(values * values, axis=0, keepdims=True) / C
    scaled = values * lax.rsqrt(power + EPS) * gain
    return (scaled * (0.5 * jnp.tanh(0.5 * scaled) + 0.5)).astype(BF16)


def kernel(
    h_hbm, shift_hbm, scale_hbm, wt_hbm, ew_hbm, w1_hbm, g1_hbm, w2_hbm, g2_hbm,
    out_ref,
    h_ref, shift_ref, scale_ref, wt_ref, g1_ref, g2_ref, w1, w2, parts, exact, stats, ewg, ewp, lat, cols, act1, raw, act2, total, gains, resid, fin,
    wsem, s_p, r_p, s_e, r_e, s_es, r_es, s_l, r_l, s_g, r_g, s_o, r_o, s_h, r_h, s_s, r_s, s_f, r_f,
):
    s, b, c = lax.axis_index("segment"), lax.axis_index("band"), lax.axis_index("chan")
    bands = lax.axis_size("band")
    up, down = lax.rem(b + 1, bands), lax.rem(b + bands - 1, bands)
    zpeers = [(s, b, lax.rem(c + d, 4)) for d in (1, 2, 3)]
    sibling = (1 - s, b, c)
    outer = (1 - s, jnp.where(s == 0, down, up), c)
    y = lax.rem(b, 4)
    apart = jnp.where(s == 0, y == 0, y == 3)
    passes = (y == 1) | (y == 2)
    goal = (2 - y, lax.rem(b + jnp.where(y == 2, 2, bands - 2), bands), c)
    skipped = lax.rem(b + jnp.where(s == 0, bands - 2, 2), bands)
    far = [(s, up, c), (1 - s, up, c), (s, down, c), (1 - s, down, c)]

    barrier = pltpu.get_barrier_semaphore()
    for peer in far + zpeers + [sibling]:
        pl.semaphore_signal(barrier, inc=1, device_id=peer, device_id_type=MESH)

    @pl.when(apart)
    def _():
        for seg in range(2):
            pl.semaphore_signal(barrier, inc=1, device_id=(seg, skipped, c), device_id_type=MESH)


    pairs = (
        (wt_hbm, wt_ref), (scale_hbm, scale_ref), (shift_hbm, shift_ref), (h_hbm, h_ref), (g1_hbm, g1_ref), (g2_hbm, g2_ref),
        (ew_hbm, ewp.at[pl.ds(0, 432)]), (w1_hbm, w1), (w2_hbm, w2),
    )
    loads = [pltpu.make_async_copy(src, dst, wsem.at[i]) for i, (src, dst) in enumerate(pairs)]
    for load in loads:
        load.start()

    def ready(src, dst, send, recv, peer):
        return pltpu.make_async_remote_copy(
            src_ref=src, dst_ref=dst, send_sem=send, recv_sem=recv, device_id=peer, device_id_type=MESH
        )

    def remote(*ends):
        copy = ready(*ends)
        copy.start()
        return copy

    sent = []

    order = iota((64, 64), 0)
    source = 4 * lax.rem(order, 16) + 2 * lax.rem(order // 16, 2) + order // 32
    permute = (iota((64, 64), 1) == source).astype(F32).astype(BF16)
    for load in loads[:3]:
        load.wait()
    weight = jnp.dot(permute, wt_ref[...], preferred_element_type=F32)
    raised = weight * (1.0 + lanes_of(scale_ref))
    high = raised.astype(BF16)
    low = (raised - high.astype(F32)).astype(BF16)
    for load in loads[3:6]:
        load.wait()
    both = lax.dot_general(jnp.concatenate([high, low], axis=0), h_ref[...], NT, preferred_element_type=F32)
    states = h_ref[...].astype(F32)
    sums = as_row(jnp.sum(states, axis=1, keepdims=True))
    lift = jnp.sum(high.astype(F32) + low.astype(F32), axis=1, keepdims=True)
    exact[...] = both[0:64] + both[64:128] - lift * (sums / 1280)
    parts[c] = exact[...].astype(BF16)
    stats[c] = jnp.zeros((8, X), F32)
    stats[c, 0:1, :] = sums
    stats[c, 1:2, :] = as_row(jnp.sum(states * states, axis=1, keepdims=True))
    stats[c, 2:3, :] = as_row(lift)
    stats[c, 3:4, :] = as_row(jnp.sum(weight * lanes_of(shift_ref), axis=1, keepdims=True))
    stats[c, 4:5, 0:OWN] = g1_ref[...]
    stats[c, 5:6, 0:OWN] = g2_ref[...]

    pl.semaphore_wait(barrier, 8 + passes.astype(jnp.int32))
    first = [remote(parts.at[c], parts.at[c], s_p.at[d], r_p.at[d], zpeers[d]) for d in (1, 0, 2)]
    first += [remote(stats.at[c], stats.at[c], s_p.at[3 + d], r_p.at[3 + d], zpeers[d]) for d in (1, 0, 2)]
    sent += first

    own_rows = pl.ds(pl.multiple_of(c * OWN, OWN), OWN)
    loads[6].wait()
    ewp[432:512, :] = jnp.zeros((80, OWN), BF16)
    eye96 = (iota((OWN, OWN), 0) == iota((OWN, OWN), 1)).astype(F32).astype(BF16)
    half = ewp[pl.ds(pl.multiple_of(s * 256, 256), 256), :]
    ewg[s, own_rows, :] = lax.dot_general(eye96, half, NT, preferred_element_type=F32).astype(BF16)
    gather_e = [
        remote(ewg.at[s, own_rows], ewg.at[s, own_rows], s_e.at[d], r_e.at[d], zpeers[d]) for d in range(3)
    ]
    sent += gather_e

    zero = jnp.zeros((16, X), BF16)
    for e in range(4):
        for f in range(4):
            at = (e * 4 + f) * X
            cols[432:512, at : at + X] = jnp.zeros((80, X), BF16)
            for p in range(2 - f):
                for qr in range(9):
                    k = (p * 9 + qr) * 16
                    cols[k : k + 16, at : at + X] = zero
        act1[e, :, 0:X] = jnp.zeros((C, X), BF16)
    for slot in range(3):
        act2[slot, :, 0:X] = jnp.zeros((C, X), BF16)

    @pl.when(~apart)
    def _():
        lat[4 * s] = jnp.zeros((4, 32, X), BF16)

    for copy in first:
        copy.wait_recv()
    summed = (stats[0] + stats[1]) + (stats[2] + stats[3])
    center = summed[0:1] / D
    spread = summed[1:2] / D - center * center
    terms = [
        jnp.where(c == chan, exact[...], parts[chan].astype(F32)) + column(stats[chan, 2:3, :], 64) * (stats[chan, 0:1, :] / 1280 - center)
        for chan in range(4)
    ]
    head = (terms[0] + terms[1]) + (terms[2] + terms[3])
    head = head * lax.rsqrt(spread + EPS) + column(summed[3:4], 64)
    head = head.astype(BF16)
    even = lax.rem(iota((32, X), 1), 2) == 0
    for t in range(2):
        spreadout = (iota((X, X), 0) == t * 64 + iota((X, X), 1) // 2).astype(F32).astype(BF16)
        wide = jnp.dot(head, spreadout, preferred_element_type=F32)
        lat[2, 2 * s + t] = jnp.where(even, wide[0:32], wide[32:64]).astype(BF16)
    mine = pl.ds(2 * s, 2)
    whole, row0, row1 = pl.ds(0, 32), pl.ds(0, 16), pl.ds(16, 16)

    def latent(slot, rows, j, arrives, peer):
        return ready(lat.at[2, mine, rows], lat.at[slot, mine, rows], s_l.at[j], r_l.at[arrives], peer)

    latents = [
        latent(1, whole, 1, 1 + s, (0, up, c)),
        latent(1, row1, 2, 1 + s, (1, up, c)),
        latent(3, row0, 3, 3 + s, (0, down, c)),
        latent(3, whole, 4, 3 + s, (1, down, c)),
        latent(2, whole, 0, 0, sibling),
    ]
    beyond = (latent(0, row1, 5, 5 + s, goal), latent(4, row0, 5, 5 + s, goal))
    for seg in range(2):
        pl.when(passes & (goal[0] == seg))(beyond[seg].start)
    for copy in latents:
        copy.start()
    sent += latents
    for chan in range(4):
        for g in range(2):
            row = stats[chan, 4 + g : 5 + g, :]
            gains[g, chan * OWN : (chan + 1) * OWN, :] = jnp.broadcast_to(column(row, OWN), (OWN, X))

    for copy in gather_e:
        copy.wait_recv()
    share = remote(ewg.at[s], ewg.at[s], s_es, r_es, sibling)
    sent.append(share)
    latents[4].wait_recv()
    for seg in range(2):

        @pl.when(s == seg)
        def _():
            for slot, rows in ((1, (whole, row1)[seg]), (3, (row0, whole)[seg])):
                for source_seg in range(2):
                    latent(slot, rows, 1, slot + source_seg, sibling).wait_recv()

        @pl.when(apart & (s == seg))
        def _():
            for source_seg in range(2):
                latent(4 * seg, (row1, row0)[seg], 5, 5 + source_seg, sibling).wait_recv()


    @pl.when(b == 0)
    def _():
        lat[1] = jnp.zeros((4, 32, X), BF16)

    @pl.when(b == bands - 1)
    def _():
        lat[3] = jnp.zeros((4, 32, X), BF16)

    lane = iota((16, X), 1)

    def windows(lo, n):
        for k in range(6):
            slot, a = s + (1 + k) // 2, (1 + k) % 2
            for f in range(lo + n):
                tile = lat[slot, f, a * 16 : a * 16 + 16, :]
                wide = tile.astype(F32)
                shifted = [
                    jnp.where(lane == 0, 0.0, pltpu.roll(wide, 1, 1)).astype(BF16),
                    tile,
                    jnp.where(lane == X - 1, 0.0, pltpu.roll(wide, X - 1, 1)).astype(BF16),
                ]
                for p in range(3):
                    for q in range(3):
                        e, g = k - q, f + 2 - p
                        if 0 <= e < 4 and lo <= g < lo + n:
                            for r in range(3):
                                row = ((p * 3 + q) * 3 + r) * 16
                                at = (e * 4 + g) * X
                                cols[row : row + 16, at : at + X] = shifted[r]

    row_at = 2 * b + 2 * s - 2

    def entry_row(e, lo, n, own=False):
        at = pl.ds(pl.multiple_of((e * 4 + lo) * X, n * X), n * X)
        value = jnp.dot(ewg[0], cols[0:256, at], preferred_element_type=F32)
        value += jnp.dot(ewg[1], cols[256:512, at], preferred_element_type=F32)
        rounded = value.astype(BF16)
        if own:
            total[0, :, 0 : n * X] = rounded.astype(F32)
            resid[:, lo * X : (lo + n) * X] = total[0, own_rows, 0 : n * X]
        valid = (row_at + e >= 0) & (row_at + e < 2 * bands)
        for t in range(n):
            done = silu_norm(rounded[:, t * X : (t + 1) * X].astype(F32), gains[0])
            lanes = (lo + t + 1) * X
            act1[e, :, lanes : lanes + X] = jnp.where(valid, done, jnp.zeros_like(done))

    def taps(weights, acts, q, lo, n, slot=None):
        slot = q if slot is None else slot
        value = None
        for p in range(max(0, 3 - lo - n), 3):
            lanes = (lo + p - 1) * X
            rows = pl.ds(pl.multiple_of((p * 3 + q) * 288, 288), 288)
            term = jnp.dot(weights[rows, :], acts[slot, :, lanes : lanes + n * X], preferred_element_type=F32)
            value = term if value is None else value + term
        return value

    lane96 = iota((OWN, X), 1)

    def join(value, t):
        lanes = slice(t * X, (t + 1) * X)
        left = jnp.where(lane96 == 0, 0.0, pltpu.roll(value[0:OWN, lanes], 1, 1))
        right = jnp.where(lane96 == X - 1, 0.0, pltpu.roll(value[2 * OWN : 3 * OWN, lanes], X - 1, 1))
        return left + value[OWN : 2 * OWN, lanes] + right

    near, away = 2 - 2 * s, 2 * s
    between = (c == 1) | (c == 2)
    relayed = 4

    class Gather:
        def __init__(self, f, slot, sends, recvs):
            tile = raw.at[slot, f, own_rows]
            self.out = [ready(tile, tile, sends.at[f, d], recvs.at[f, c], zpeers[d]) for d in range(3)]
            self.into = [
                ready(tile, tile, sends.at[f, d], recvs.at[f, lax.rem(c + d + 1, 4)], zpeers[d]) for d in range(3)
            ]
            self.direct = [c != 3, None, c != 0] if f < relayed else [None, None, None]
            source = 3 * (2 - c)
            end = raw.at[slot, f, pl.ds(pl.multiple_of(jnp.where(between, source, c) * OWN, OWN), OWN)]
            self.relay = None
            if f < relayed:
                goal_chan = jnp.where(between, 3 * (c - 1), lax.rem(c + 1, 4))
                self.relay = ready(
                    end, end, sends.at[f, 3], recvs.at[f, jnp.where(between, source, c)], (s, b, goal_chan)
                )

        def start(self):
            for copy, when in zip(self.out, self.direct):
                if when is None:
                    copy.start()
                else:
                    pl.when(when)(copy.start)

        def arrive(self):
            self.into[1].wait_recv()
            if self.relay is not None:
                pl.when(between)(self.relay.start)
            self.into[0].wait_recv()
            self.into[2].wait_recv()

        def sent(self):
            for copy, when in zip(self.out, self.direct):
                if when is None:
                    copy.wait_send()
                else:
                    pl.when(when)(copy.wait_send)
            if self.relay is not None:
                pl.when(between)(self.relay.wait_send)

    own_gather = [Gather(f, 1, s_g, r_g) for f in range(4)]
    halo = [Gather(f, away, s_h, r_h) for f in range(4)]
    to_sibling = [ready(raw.at[1, f], raw.at[away, f], s_s.at[f], r_s.at[f], sibling) for f in range(4)]
    across = [ready(raw.at[1, f], raw.at[near, f], s_o.at[f], r_o.at[f], outer) for f in range(4)]

    def middle_row(start, slot, lo, n, copies):
        value = None
        for q in range(3):
            term = taps(w1, act1, q, lo, n, start + q)
            value = term if value is None else value + term
        for t in range(n):
            f = lo + t
            raw[slot, f, own_rows, :] = join(value, t).astype(BF16)
            copies[f].start()

    for lo, n in ((0, 2), (2, 2)):
        windows(lo, n)
        if lo == 0:
            share.wait_recv()
        for k in range(3):
            entry_row(1 - s + k, lo, n, own=k == 1)
        if lo == 0:
            loads[7].wait()
        middle_row(1 - s, 1, lo, n, own_gather)

        @pl.when(apart)
        def _():
            entry_row(3 * s, lo, n)
            middle_row(s, away, lo, n, halo)

    def activate(slot, f, valid):
        done = silu_norm(raw[slot, f].astype(F32), gains[1])
        lanes = (f + 1) * X
        act2[slot, :, lanes : lanes + X] = jnp.where(valid, done, jnp.zeros_like(done))

    inside = jnp.where(s == 0, b > 0, b < bands - 1)

    def own_arrives(f):
        own_gather[f].arrive()
        to_sibling[f].start()
        pl.when(~apart)(across[f].start)

    def away_arrives(f):
        pl.when(apart)(halo[f].arrive)
        pl.when(~apart)(across[f].wait_recv)
        activate(away, f, inside)

    sections = [ready(fin.at[0, f], fin.at[1, f], s_f.at[f], r_f.at[f], sibling) for f in range(4)]

    def decode(pair, value):
        for t in range(2):
            f = pair * 2 + t
            fin[0, f] = (resid[:, f * X : (f + 1) * X] + join(value, t)).astype(BF16)
            pl.when(s == 1 - pair)(sections[f].start)

    own_arrives(0)
    own_arrives(1)
    activate(1, 0, True)
    activate(1, 1, True)
    loads[8].wait()
    total[0, 0:288, :] = taps(w2, act2, 1, 0, 2)
    for f in range(2):
        to_sibling[f].wait_recv()
        activate(near, f, True)
    total[0, 0:288, :] += taps(w2, act2, near, 0, 2)
    own_arrives(2)
    own_arrives(3)
    for f in range(2):
        away_arrives(f)
    decode(0, total[0, 0:288, :] + taps(w2, act2, away, 0, 2))
    activate(1, 2, True)
    activate(1, 3, True)
    total[1, 0:288, :] = taps(w2, act2, 1, 2, 2)
    for f in (2, 3):
        to_sibling[f].wait_recv()
        activate(near, f, True)
    total[1, 0:288, :] += taps(w2, act2, near, 2, 2)
    for f in (2, 3):
        away_arrives(f)
    decode(1, total[1, 0:288, :] + taps(w2, act2, away, 2, 2))
    for t in range(2):
        out_ref[t, s] = fin[0, 2 * s + t]
    for t in range(2):
        for seg in range(2):
            pl.when(s == seg)(sections[2 * seg + t].wait_recv)
        out_ref[t, 1 - s] = fin[1, 2 * s + t]
    for seg in range(2):
        pl.when(passes & (goal[0] == seg))(beyond[seg].wait_send)
    for f in range(4):
        pl.when(s == 1 - f // 2)(sections[f].wait_send)
    for copy in sent + to_sibling:
        copy.wait_send()
    for gather in own_gather:
        gather.sent()

    @pl.when(apart)
    def _():
        for gather in halo:
            gather.sent()

    @pl.when(~apart)
    def _():
        for copy in across:
            copy.wait_send()


def body(
    hidden_states, modulation_shift, modulation_scale, head_weight, entry_weight,
    first_weight, first_gain, second_weight, second_gain,
):
    vmem = pl.BlockSpec(memory_space=pltpu.VMEM)
    hbm = pl.BlockSpec(memory_space=pltpu.HBM)
    dma = pltpu.SemaphoreType.DMA
    out = pl.pallas_call(
        kernel,
        out_shape=pltpu.VMEM((2, 2, OWN, X), BF16),
        in_specs=[hbm] * 9,
        out_specs=vmem,
        scratch_shapes=[
            pltpu.VMEM((128, 1280), BF16),
            pltpu.VMEM((10, X), F32),
            pltpu.VMEM((10, X), F32),
            pltpu.VMEM((64, 1280), BF16),
            pltpu.VMEM((1, OWN), F32),
            pltpu.VMEM((1, OWN), F32),
            pltpu.VMEM((2592, C), BF16),
            pltpu.VMEM((2592, C), BF16),
            pltpu.VMEM((4, 64, X), BF16),
            pltpu.VMEM((64, X), F32),
            pltpu.VMEM((4, 8, X), F32),
            pltpu.VMEM((2, C, 256), BF16),
            pltpu.VMEM((512, OWN), BF16),
            pltpu.VMEM((5, 4, 32, X), BF16),
            pltpu.VMEM((512, 16 * X), BF16),
            pltpu.VMEM((4, C, 5 * X), BF16),
            pltpu.VMEM((3, 4, C, X), BF16),
            pltpu.VMEM((3, C, 5 * X), BF16),
            pltpu.VMEM((2, C, 2 * X), F32),
            pltpu.VMEM((2, C, X), F32),
            pltpu.VMEM((OWN, 4 * X), F32),
            pltpu.VMEM((2, 4, OWN, X), BF16),
            dma((9,)), dma((6,)), dma((6,)), dma((3,)), dma((3,)), dma, dma, dma((6,)), dma((7,)),
            dma((4, 4)), dma((4, 4)), dma((4,)), dma((4,)), dma((4, 4)), dma((4, 4)), dma((4,)), dma((4,)),
            dma((4,)), dma((4,)),
        ],
        compiler_params=pltpu.CompilerParams(
            collective_id=0, has_side_effects=True, vmem_limit_bytes=60 * 10**6
        ),
    )(
        hidden_states.reshape(128, 1280),
        modulation_shift.reshape(10, X),
        modulation_scale.reshape(10, X),
        head_weight.T,
        entry_weight.transpose(0, 1, 2, 4, 3).reshape(432, OWN),
        first_weight.reshape(2592, C),
        first_gain.reshape(1, OWN),
        second_weight.reshape(2592, C),
        second_gain.reshape(1, OWN),
    )
    return out.transpose(2, 0, 1, 3)


def solution(mesh):
    return jax.shard_map(
        body,
        mesh=mesh,
        in_specs=(
            P("segment", "band", None, "chan"),
            P("chan"),
            P("chan"),
            P("chan", None),
            P(None, None, None, "chan", None),
            P(None, None, None, "chan", None),
            P("chan"),
            P(None, None, None, "chan", None),
            P("chan"),
        ),
        out_specs=P("chan", "segment", "band", None),
        check_vma=False,
    )
```

```python
import jax
import jax.numpy as jnp
from jax import lax
from jax.experimental import pallas as pl
from jax.experimental.pallas import tpu as pltpu
from jax.sharding import PartitionSpec as P

D = 5120
C = 384
EPS = 1e-6
OWN = 96
X = 128
MESH = pl.DeviceIdType.MESH
NT = (((1,), (1,)), ((), ()))
F32 = jnp.float32
BF16 = jnp.bfloat16


def iota(shape, axis):
    return lax.broadcasted_iota(jnp.int32, shape, axis)


def column(row, rows):
    eye = iota((rows, X), 0) == iota((rows, X), 1)
    return jnp.sum(jnp.where(eye, jnp.broadcast_to(row, (rows, X)), 0.0), axis=1, keepdims=True)


def as_row(col):
    rows = col.shape[0]
    eye = iota((rows, X), 0) == iota((rows, X), 1)
    return jnp.sum(jnp.where(eye, jnp.broadcast_to(col, (rows, X)), 0.0), axis=0, keepdims=True)


def lanes_of(ref):
    return jnp.concatenate([ref[j : j + 1, :] for j in range(10)], axis=1)


def silu_norm(values, gain):
    power = jnp.sum(values * values, axis=0, keepdims=True) / C
    scaled = values * lax.rsqrt(power + EPS) * gain
    return (scaled * (0.5 * jnp.tanh(0.5 * scaled) + 0.5)).astype(BF16)


def kernel(
    h_hbm, shift_hbm, scale_hbm, wt_hbm, ew_hbm, w1_hbm, g1_hbm, w2_hbm, g2_hbm,
    out_ref,
    h_ref, shift_ref, scale_ref, wt_ref, g1_ref, g2_ref, w1, w2, parts, exact, stats, ewg, ewp, lat, cols, act1, raw, act2, total, gains, resid, fin,
    wsem, s_p, r_p, s_e, r_e, s_es, r_es, s_l, r_l, s_g, r_g, s_o, r_o, s_h, r_h, s_s, r_s, s_f, r_f,
):
    s, b, c = lax.axis_index("segment"), lax.axis_index("band"), lax.axis_index("chan")
    bands = lax.axis_size("band")
    up, down = lax.rem(b + 1, bands), lax.rem(b + bands - 1, bands)
    zpeers = [(s, b, lax.rem(c + d, 4)) for d in (1, 2, 3)]
    sibling = (1 - s, b, c)
    outer = (1 - s, jnp.where(s == 0, down, up), c)
    y = lax.rem(b, 4)
    apart = jnp.where(s == 0, y == 0, y == 3)
    passes = (y == 1) | (y == 2)
    goal = (2 - y, lax.rem(b + jnp.where(y == 2, 2, bands - 2), bands), c)
    skipped = lax.rem(b + jnp.where(s == 0, bands - 2, 2), bands)
    far = [(s, up, c), (1 - s, up, c), (s, down, c), (1 - s, down, c)]

    barrier = pltpu.get_barrier_semaphore()
    for peer in far + zpeers + [sibling]:
        pl.semaphore_signal(barrier, inc=1, device_id=peer, device_id_type=MESH)

    @pl.when(apart)
    def _():
        for seg in range(2):
            pl.semaphore_signal(barrier, inc=1, device_id=(seg, skipped, c), device_id_type=MESH)


    pairs = (
        (wt_hbm, wt_ref), (scale_hbm, scale_ref), (shift_hbm, shift_ref), (h_hbm, h_ref), (g1_hbm, g1_ref), (g2_hbm, g2_ref),
        (ew_hbm, ewp.at[pl.ds(0, 432)]), (w1_hbm, w1), (w2_hbm, w2),
    )
    loads = [pltpu.make_async_copy(src, dst, wsem.at[i]) for i, (src, dst) in enumerate(pairs)]
    for load in loads:
        load.start()

    def ready(src, dst, send, recv, peer):
        return pltpu.make_async_remote_copy(
            src_ref=src, dst_ref=dst, send_sem=send, recv_sem=recv, device_id=peer, device_id_type=MESH
        )

    def remote(*ends):
        copy = ready(*ends)
        copy.start()
        return copy

    sent = []

    order = iota((64, 64), 0)
    source = 4 * lax.rem(order, 16) + 2 * lax.rem(order // 16, 2) + order // 32
    permute = (iota((64, 64), 1) == source).astype(F32).astype(BF16)
    for load in loads[:3]:
        load.wait()
    weight = jnp.dot(permute, wt_ref[...], preferred_element_type=F32)
    raised = weight * (1.0 + lanes_of(scale_ref))
    high = raised.astype(BF16)
    low = (raised - high.astype(F32)).astype(BF16)
    lift = jnp.sum(high.astype(F32) + low.astype(F32), axis=1, keepdims=True)
    stats[c] = jnp.zeros((8, X), F32)
    stats[c, 2:3, :] = as_row(lift)
    stats[c, 3:4, :] = as_row(jnp.sum(weight * lanes_of(shift_ref), axis=1, keepdims=True))
    for load in loads[3:6]:
        load.wait()
    stats[c, 4:5, 0:OWN] = g1_ref[...]
    stats[c, 5:6, 0:OWN] = g2_ref[...]
    both = lax.dot_general(jnp.concatenate([high, low], axis=0), h_ref[...], NT, preferred_element_type=F32)
    states = h_ref[...].astype(F32)
    sums = as_row(jnp.sum(states, axis=1, keepdims=True))
    stats[c, 0:1, :] = sums
    stats[c, 1:2, :] = as_row(jnp.sum(states * states, axis=1, keepdims=True))
    exact[...] = both[0:64] + both[64:128] - lift * (sums / 1280)
    parts[c] = exact[...].astype(BF16)

    pl.semaphore_wait(barrier, 8 + passes.astype(jnp.int32))
    first = [remote(parts.at[c], parts.at[c], s_p.at[d], r_p.at[d], zpeers[d]) for d in (1, 0, 2)]
    first += [remote(stats.at[c], stats.at[c], s_p.at[3 + d], r_p.at[3 + d], zpeers[d]) for d in (1, 0, 2)]
    own_rows = pl.ds(pl.multiple_of(c * OWN, OWN), OWN)
    loads[6].wait()
    ewp[432:512, :] = jnp.zeros((80, OWN), BF16)
    eye96 = (iota((OWN, OWN), 0) == iota((OWN, OWN), 1)).astype(F32).astype(BF16)
    half = ewp[pl.ds(pl.multiple_of(s * 256, 256), 256), :]
    ewg[s, own_rows, :] = lax.dot_general(eye96, half, NT, preferred_element_type=F32).astype(BF16)
    for copy in first:
        copy.wait_send()
    gather_e = [
        remote(ewg.at[s, own_rows], ewg.at[s, own_rows], s_e.at[d], r_e.at[d], zpeers[d]) for d in range(3)
    ]
    sent += gather_e

    zero = jnp.zeros((16, X), BF16)
    for e in range(4):
        for f in range(4):
            at = (e * 4 + f) * X
            cols[432:512, at : at + X] = jnp.zeros((80, X), BF16)
            for p in range(2 - f):
                for qr in range(9):
                    k = (p * 9 + qr) * 16
                    cols[k : k + 16, at : at + X] = zero
        act1[e, :, 0:X] = jnp.zeros((C, X), BF16)
    for slot in range(3):
        act2[slot, :, 0:X] = jnp.zeros((C, X), BF16)

    @pl.when(~apart)
    def _():
        lat[4 * s] = jnp.zeros((4, 32, X), BF16)

    for copy in first:
        copy.wait_recv()
    summed = (stats[0] + stats[1]) + (stats[2] + stats[3])
    center = summed[0:1] / D
    spread = summed[1:2] / D - center * center
    terms = [
        jnp.where(c == chan, exact[...], parts[chan].astype(F32)) + column(stats[chan, 2:3, :], 64) * (stats[chan, 0:1, :] / 1280 - center)
        for chan in range(4)
    ]
    head = (terms[0] + terms[1]) + (terms[2] + terms[3])
    head = head * lax.rsqrt(spread + EPS) + column(summed[3:4], 64)
    head = head.astype(BF16)
    even = lax.rem(iota((32, X), 1), 2) == 0
    for t in range(2):
        spreadout = (iota((X, X), 0) == t * 64 + iota((X, X), 1) // 2).astype(F32).astype(BF16)
        wide = jnp.dot(head, spreadout, preferred_element_type=F32)
        lat[2, 2 * s + t] = jnp.where(even, wide[0:32], wide[32:64]).astype(BF16)
    mine = pl.ds(2 * s, 2)
    whole, row0, row1 = pl.ds(0, 32), pl.ds(0, 16), pl.ds(16, 16)

    def latent(slot, rows, j, arrives, peer):
        return ready(lat.at[2, mine, rows], lat.at[slot, mine, rows], s_l.at[j], r_l.at[arrives], peer)

    latents = [
        latent(1, whole, 1, 1 + s, (0, up, c)),
        latent(1, row1, 2, 1 + s, (1, up, c)),
        latent(3, row0, 3, 3 + s, (0, down, c)),
        latent(3, whole, 4, 3 + s, (1, down, c)),
        latent(2, whole, 0, 0, sibling),
    ]
    beyond = (latent(0, row1, 5, 5 + s, goal), latent(4, row0, 5, 5 + s, goal))
    for seg in range(2):
        pl.when(passes & (goal[0] == seg))(beyond[seg].start)
    for copy in latents:
        copy.start()
    sent += latents
    for chan in range(4):
        for g in range(2):
            row = stats[chan, 4 + g : 5 + g, :]
            gains[g, chan * OWN : (chan + 1) * OWN, :] = jnp.broadcast_to(column(row, OWN), (OWN, X))

    for copy in gather_e:
        copy.wait_recv()
    share = remote(ewg.at[s], ewg.at[s], s_es, r_es, sibling)
    sent.append(share)
    latents[4].wait_recv()
    for seg in range(2):

        @pl.when(s == seg)
        def _():
            for slot, rows in ((1, (whole, row1)[seg]), (3, (row0, whole)[seg])):
                for source_seg in range(2):
                    latent(slot, rows, 1, slot + source_seg, sibling).wait_recv()

        @pl.when(apart & (s == seg))
        def _():
            for source_seg in range(2):
                latent(4 * seg, (row1, row0)[seg], 5, 5 + source_seg, sibling).wait_recv()


    @pl.when(b == 0)
    def _():
        lat[1] = jnp.zeros((4, 32, X), BF16)

    @pl.when(b == bands - 1)
    def _():
        lat[3] = jnp.zeros((4, 32, X), BF16)

    lane = iota((16, X), 1)

    def windows(lo, n):
        for k in range(6):
            slot, a = s + (1 + k) // 2, (1 + k) % 2
            for f in range(lo + n):
                tile = lat[slot, f, a * 16 : a * 16 + 16, :]
                wide = tile.astype(F32)
                shifted = [
                    jnp.where(lane == 0, 0.0, pltpu.roll(wide, 1, 1)).astype(BF16),
                    tile,
                    jnp.where(lane == X - 1, 0.0, pltpu.roll(wide, X - 1, 1)).astype(BF16),
                ]
                for p in range(3):
                    for q in range(3):
                        e, g = k - q, f + 2 - p
                        if 0 <= e < 4 and lo <= g < lo + n:
                            for r in range(3):
                                row = ((p * 3 + q) * 3 + r) * 16
                                at = (e * 4 + g) * X
                                cols[row : row + 16, at : at + X] = shifted[r]

    row_at = 2 * b + 2 * s - 2

    def entry_row(e, lo, n, own=False):
        at = pl.ds(pl.multiple_of((e * 4 + lo) * X, n * X), n * X)
        value = jnp.dot(ewg[0], cols[0:256, at], preferred_element_type=F32)
        value += jnp.dot(ewg[1], cols[256:512, at], preferred_element_type=F32)
        rounded = value.astype(BF16)
        if own:
            total[0, :, 0 : n * X] = rounded.astype(F32)
            resid[:, lo * X : (lo + n) * X] = total[0, own_rows, 0 : n * X]
        valid = (row_at + e >= 0) & (row_at + e < 2 * bands)
        for t in range(n):
            done = silu_norm(rounded[:, t * X : (t + 1) * X].astype(F32), gains[0])
            lanes = (lo + t + 1) * X
            act1[e, :, lanes : lanes + X] = jnp.where(valid, done, jnp.zeros_like(done))

    def taps(weights, acts, q, lo, n, slot=None):
        slot = q if slot is None else slot
        value = None
        for p in range(max(0, 3 - lo - n), 3):
            lanes = (lo + p - 1) * X
            rows = pl.ds(pl.multiple_of((p * 3 + q) * 288, 288), 288)
            term = jnp.dot(weights[rows, :], acts[slot, :, lanes : lanes + n * X], preferred_element_type=F32)
            value = term if value is None else value + term
        return value

    lane96 = iota((OWN, X), 1)

    def join(value, t):
        lanes = slice(t * X, (t + 1) * X)
        left = jnp.where(lane96 == 0, 0.0, pltpu.roll(value[0:OWN, lanes], 1, 1))
        right = jnp.where(lane96 == X - 1, 0.0, pltpu.roll(value[2 * OWN : 3 * OWN, lanes], X - 1, 1))
        return left + value[OWN : 2 * OWN, lanes] + right

    near, away = 2 - 2 * s, 2 * s
    between = (c == 1) | (c == 2)
    relayed = 4

    class Gather:
        def __init__(self, f, slot, sends, recvs):
            tile = raw.at[slot, f, own_rows]
            self.out = [ready(tile, tile, sends.at[f, d], recvs.at[f, c], zpeers[d]) for d in range(3)]
            self.into = [
                ready(tile, tile, sends.at[f, d], recvs.at[f, lax.rem(c + d + 1, 4)], zpeers[d]) for d in range(3)
            ]
            self.direct = [c != 3, None, c != 0] if f < relayed else [None, None, None]
            source = 3 * (2 - c)
            end = raw.at[slot, f, pl.ds(pl.multiple_of(jnp.where(between, source, c) * OWN, OWN), OWN)]
            self.relay = None
            if f < relayed:
                goal_chan = jnp.where(between, 3 * (c - 1), lax.rem(c + 1, 4))
                self.relay = ready(
                    end, end, sends.at[f, 3], recvs.at[f, jnp.where(between, source, c)], (s, b, goal_chan)
                )

        def start(self):
            for copy, when in zip(self.out, self.direct):
                if when is None:
                    copy.start()
                else:
                    pl.when(when)(copy.start)

        def arrive(self):
            self.into[1].wait_recv()
            if self.relay is not None:
                pl.when(between)(self.relay.start)
            self.into[0].wait_recv()
            self.into[2].wait_recv()

        def relayed(self):
            if self.relay is not None:
                pl.when(between)(self.relay.wait_send)

        def sent(self):
            for copy, when in zip(self.out, self.direct):
                if when is None:
                    copy.wait_send()
                else:
                    pl.when(when)(copy.wait_send)

    own_gather = [Gather(f, 1, s_g, r_g) for f in range(4)]
    halo = [Gather(f, away, s_h, r_h) for f in range(4)]
    to_sibling = [ready(raw.at[1, f], raw.at[away, f], s_s.at[f], r_s.at[f], sibling) for f in range(4)]
    across = [ready(raw.at[1, f], raw.at[near, f], s_o.at[f], r_o.at[f], outer) for f in range(4)]

    def middle_row(start, slot, lo, n, copies):
        value = None
        for q in range(3):
            term = taps(w1, act1, q, lo, n, start + q)
            value = term if value is None else value + term
        for t in range(n):
            f = lo + t
            raw[slot, f, own_rows, :] = join(value, t).astype(BF16)
            copies[f].start()

    for lo, n in ((0, 2), (2, 2)):
        windows(lo, n)
        if lo == 0:
            share.wait_recv()
        for k in range(3):
            entry_row(1 - s + k, lo, n, own=k == 1)
        if lo == 0:
            loads[7].wait()
        middle_row(1 - s, 1, lo, n, own_gather)

        @pl.when(apart)
        def _():
            entry_row(3 * s, lo, n)
            middle_row(s, away, lo, n, halo)

    def activate(slot, f, valid):
        done = silu_norm(raw[slot, f].astype(F32), gains[1])
        lanes = (f + 1) * X
        act2[slot, :, lanes : lanes + X] = jnp.where(valid, done, jnp.zeros_like(done))

    inside = jnp.where(s == 0, b > 0, b < bands - 1)

    def own_arrives(f):
        own_gather[f].arrive()
        to_sibling[f].start()
        pl.when(~apart)(across[f].start)

    def away_arrives(f):
        pl.when(apart)(halo[f].arrive)
        pl.when(~apart)(across[f].wait_recv)
        activate(away, f, inside)

    sections = [ready(fin.at[0, f], fin.at[1, f], s_f.at[f], r_f.at[f], sibling) for f in range(4)]

    def decode(pair, value):
        for t in range(2):
            f = pair * 2 + t
            fin[0, f] = (resid[:, f * X : (f + 1) * X] + join(value, t)).astype(BF16)
            pl.when(s == 1 - pair)(sections[f].start)

    own_arrives(0)
    own_arrives(1)
    activate(1, 0, True)
    activate(1, 1, True)
    loads[8].wait()
    total[0, 0:288, :] = taps(w2, act2, 1, 0, 2)
    for f in range(2):
        to_sibling[f].wait_recv()
        activate(near, f, True)
    total[0, 0:288, :] += taps(w2, act2, near, 0, 2)
    own_arrives(2)
    own_arrives(3)
    for f in range(2):
        away_arrives(f)
    decode(0, total[0, 0:288, :] + taps(w2, act2, away, 0, 2))
    activate(1, 2, True)
    activate(1, 3, True)
    total[1, 0:288, :] = taps(w2, act2, 1, 2, 2)
    for f in (2, 3):
        to_sibling[f].wait_recv()
        activate(near, f, True)
    total[1, 0:288, :] += taps(w2, act2, near, 2, 2)
    for seg in range(2):
        pl.when(passes & (goal[0] == seg))(beyond[seg].wait_send)
    for copy in sent + to_sibling:
        copy.wait_send()
    for gather in own_gather:
        gather.sent()
        gather.relayed()

    @pl.when(apart)
    def _():
        for gather in halo:
            gather.sent()

    @pl.when(~apart)
    def _():
        for copy in across:
            copy.wait_send()

    for f in (2, 3):
        away_arrives(f)
    decode(1, total[1, 0:288, :] + taps(w2, act2, away, 2, 2))
    for t in range(2):
        out_ref[t, s] = fin[0, 2 * s + t]
    for t in range(2):
        for seg in range(2):
            pl.when(s == seg)(sections[2 * seg + t].wait_recv)
        out_ref[t, 1 - s] = fin[1, 2 * s + t]
    for f in range(4):
        pl.when(s == 1 - f // 2)(sections[f].wait_send)

    @pl.when(apart)
    def _():
        for gather in halo:
            gather.relayed()


def body(
    hidden_states, modulation_shift, modulation_scale, head_weight, entry_weight,
    first_weight, first_gain, second_weight, second_gain,
):
    vmem = pl.BlockSpec(memory_space=pltpu.VMEM)
    hbm = pl.BlockSpec(memory_space=pltpu.HBM)
    dma = pltpu.SemaphoreType.DMA
    out = pl.pallas_call(
        kernel,
        out_shape=pltpu.VMEM((2, 2, OWN, X), BF16),
        in_specs=[hbm] * 9,
        out_specs=vmem,
        scratch_shapes=[
            pltpu.VMEM((128, 1280), BF16),
            pltpu.VMEM((10, X), F32),
            pltpu.VMEM((10, X), F32),
            pltpu.VMEM((64, 1280), BF16),
            pltpu.VMEM((1, OWN), F32),
            pltpu.VMEM((1, OWN), F32),
            pltpu.VMEM((2592, C), BF16),
            pltpu.VMEM((2592, C), BF16),
            pltpu.VMEM((4, 64, X), BF16),
            pltpu.VMEM((64, X), F32),
            pltpu.VMEM((4, 8, X), F32),
            pltpu.VMEM((2, C, 256), BF16),
            pltpu.VMEM((512, OWN), BF16),
            pltpu.VMEM((5, 4, 32, X), BF16),
            pltpu.VMEM((512, 16 * X), BF16),
            pltpu.VMEM((4, C, 5 * X), BF16),
            pltpu.VMEM((3, 4, C, X), BF16),
            pltpu.VMEM((3, C, 5 * X), BF16),
            pltpu.VMEM((2, C, 2 * X), F32),
            pltpu.VMEM((2, C, X), F32),
            pltpu.VMEM((OWN, 4 * X), F32),
            pltpu.VMEM((2, 4, OWN, X), BF16),
            dma((9,)), dma((6,)), dma((6,)), dma((3,)), dma((3,)), dma, dma, dma((6,)), dma((7,)),
            dma((4, 4)), dma((4, 4)), dma((4,)), dma((4,)), dma((4, 4)), dma((4, 4)), dma((4,)), dma((4,)),
            dma((4,)), dma((4,)),
        ],
        compiler_params=pltpu.CompilerParams(
            collective_id=0, has_side_effects=True, vmem_limit_bytes=60 * 10**6
        ),
    )(
        hidden_states.reshape(128, 1280),
        modulation_shift.reshape(10, X),
        modulation_scale.reshape(10, X),
        head_weight.T,
        entry_weight.transpose(0, 1, 2, 4, 3).reshape(432, OWN),
        first_weight.reshape(2592, C),
        first_gain.reshape(1, OWN),
        second_weight.reshape(2592, C),
        second_gain.reshape(1, OWN),
    )
    return out.transpose(2, 0, 1, 3)


def solution(mesh):
    return jax.shard_map(
        body,
        mesh=mesh,
        in_specs=(
            P("segment", "band", None, "chan"),
            P("chan"),
            P("chan"),
            P("chan", None),
            P(None, None, None, "chan", None),
            P(None, None, None, "chan", None),
            P("chan"),
            P(None, None, None, "chan", None),
            P("chan"),
        ),
        out_specs=P("chan", "segment", "band", None),
        check_vma=False,
    )
```
